32 devices in a mesh: ctx: 8 (over z, x), dp: 4 (over y, core).
Axes of the slice: x: 2, y: 2, z: 4, core: 2. Of those that a mesh axis runs over, the one named last changes fastest.
Arguments:
- queries: bfloat16 [4, 1024, 2048], P('dp', 'ctx'), may hold values from -400 to 400
- keys: bfloat16 [4, 1024, 1024], P('dp', 'ctx'), may hold values from -400 to 400
- values: bfloat16 [4, 1024, 1024], P('dp', 'ctx'), may hold values from -6 to 6
- q_gain: float32 [256], replicated, may hold values from 0.25 to 1.75
- key_norm_gain: float32 [256], replicated, may hold values from 0.25 to 1.75
- segment_ids: int32 [4, 1024], P('dp', 'ctx'), may hold values from 0 to 3, never falling along the last dimension, each value on 1 to 512 neighbouring positions
- output_gradient: bfloat16 [4, 1024, 2048], P('dp', 'ctx'), may hold values from -14 to 14
Outputs:
- attn_out: bfloat16 [4, 1024, 2048], P('dp', 'ctx')
- grad_queries: bfloat16 [4, 1024, 2048], P('dp', 'ctx')
- key_gradient: bfloat16 [4, 1024, 1024], P('dp', 'ctx')
- value_gradient: bfloat16 [4, 1024, 1024], P('dp', 'ctx')
- grad_q_gain: float32 [256], replicated
- grad_k_gain: float32 [256], replicated
The draws below stay inside these ranges and needn't reach their ends.
Inputs may be any that keep to these rules, and one draw needn't show every extreme that they name: `segment_ids`: document ids never fall along a sequence; every id from 0 to 3 is used, each document holds 1 to 512 tokens and at least one holds exactly 512.
All inputs are finite; a program needn't handle non-finite values.
Results may differ from the reference program's by a relative error of at most 0.013.
Values may be sent and summed in bfloat16 or wider, within the bound.
A program may use at most 64 MiB of HBM per device.

```python
import math
from functools import partial
import jax
import jax.numpy as jnp
import numpy as np
from jax import lax

QUERY_HEADS = 8
KEY_VALUE_HEADS = 4
HEAD_SIZE = 256
WINDOW = 256
DEVICE_TOKENS = 128
HALO = 2
SEQUENCE_LENGTH = 1024
SEQUENCE_COUNT = 4
DOCS = 4
DOC_MOST = 512
N_CTX = 8


def scaled_gradient_field(key, width):
    noise_key, col_key, row_key = jax.random.split(key, 3)
    shape = (SEQUENCE_COUNT, SEQUENCE_LENGTH, width)
    col_scale = jnp.exp(jax.random.uniform(col_key, (width,), jnp.float32, 0.0, math.log(10.0)))
    row_scale = jnp.exp(jax.random.uniform(row_key, (SEQUENCE_COUNT, SEQUENCE_LENGTH, 1), jnp.float32, 0.0, math.log(10.0)))
    base = jnp.clip(jax.random.normal(noise_key, shape, jnp.float32), -4.0, 4.0)
    return base * row_scale * col_scale


def draw_queries(key, part):
    return scaled_gradient_field(jax.random.fold_in(key, 11), QUERY_HEADS * HEAD_SIZE).astype(jnp.bfloat16)


def draw_keys(key, part):
    return scaled_gradient_field(jax.random.fold_in(key, 23), KEY_VALUE_HEADS * HEAD_SIZE).astype(jnp.bfloat16)


def draw_output_gradient(key, part):
    noise_key = jax.random.fold_in(jax.random.fold_in(key, 37), 0)
    shape = (SEQUENCE_COUNT, SEQUENCE_LENGTH, QUERY_HEADS * HEAD_SIZE)
    where_along = jnp.arange(SEQUENCE_LENGTH, dtype=jnp.float32).reshape(1, SEQUENCE_LENGTH, 1) / (SEQUENCE_LENGTH - 1)
    base = jnp.clip(jax.random.normal(noise_key, shape, jnp.float32), -4.0, 4.0)
    ramp = 1.0 + 2.0 * where_along
    return (base * ramp).astype(jnp.bfloat16)


def level_of(rng, extent, cuts, smallest, high):
    level = 1.0
    for dim, blocks in cuts:
        heights = jax.random.uniform(jax.random.fold_in(jax.random.fold_in(rng, 6), dim), (blocks,), jnp.float32, smallest / len(cuts), high / len(cuts))
        level = level * jnp.repeat(jnp.exp(heights), extent[dim] // blocks).reshape((-1,) + (1,) * (len(extent) - 1 - dim))
    return level


def profile(number_of, total, reach, lean):
    loads = [(1 << 20) // math.isqrt(grade ** lean) + 1 for grade in range(2, number_of + 1)]
    rest, counts = total - reach - (number_of - 1), [1] * (number_of - 1)
    while rest > 0:
        candidates = [i for i in range(number_of - 1) if counts[i] < reach]
        whole, left = sum([loads[i] for i in candidates]), rest
        for i in candidates:
            more = min(reach - counts[i], max(1, left * loads[i] // whole), rest)
            counts[i] = counts[i] + more
            rest = rest - more
    return np.array([reach] + counts)


def uneven(rng, count, total, limit, slope):
    if count == 2:
        one = jax.random.randint(rng, (), max(1, total - limit), min(limit, total - 1) + 1)
        return jnp.stack([one, total - one])
    lengths = jnp.asarray(profile(count, total, limit, slope), jnp.int32)
    pairs = (count - 1) // 2
    giver, taker = lengths[1:1 + 2 * pairs:2], lengths[2:2 + 2 * pairs:2]
    slack = jnp.minimum(giver - 1, limit - taker)
    passed = jax.random.randint(jax.random.fold_in(rng, 1), (pairs,), 0, 1 << 20) % (slack + 1)
    lengths = lengths.at[1:1 + 2 * pairs:2].set(giver - passed).at[2:2 + 2 * pairs:2].set(taker + passed)
    return lengths[jax.random.permutation(jax.random.fold_in(rng, 2), count)]


def scatter_about(own_key, extent, deviation, bound, cuts=(), held_as=jnp.bfloat16):
    gain = level_of(own_key, extent, cuts, -0.22, 0.18) if cuts else 1.0
    array = jax.random.normal(own_key, extent, jnp.float32) * deviation * gain
    return jnp.minimum(jnp.maximum(array, -bound), bound).astype(held_as)


def setup_inputs(seed: int = 0) -> dict:
    arg_keys = jax.random.split(jax.random.key(seed), 8)
    queries = draw_queries(jax.random.fold_in(arg_keys[7], 71), 0)
    keys = draw_keys(jax.random.fold_in(arg_keys[7], 71), 0)
    values = scatter_about(arg_keys[2], (SEQUENCE_COUNT, SEQUENCE_LENGTH, KEY_VALUE_HEADS * HEAD_SIZE), 1.0, 6.0, ((0, 4), (1, 8)))
    q_gain = jnp.clip(1.0 + 0.15 * jax.random.normal(arg_keys[3], (HEAD_SIZE,), jnp.float32), 0.25, 1.75)
    key_norm_gain = jnp.clip(1.0 + 0.15 * jax.random.normal(arg_keys[4], (HEAD_SIZE,), jnp.float32), 0.25, 1.75)
    segment_ids = jax.vmap(lambda own: jnp.searchsorted(jnp.cumsum(uneven(own, DOCS, SEQUENCE_LENGTH, DOC_MOST, 2)), jnp.arange(SEQUENCE_LENGTH), side="right"))(jax.random.split(arg_keys[5], SEQUENCE_COUNT)).reshape((SEQUENCE_COUNT, SEQUENCE_LENGTH)).astype(jnp.int32)
    output_gradient = draw_output_gradient(jax.random.fold_in(arg_keys[7], 71), 0)
    return dict(queries=queries, keys=keys, values=values, q_gain=q_gain, key_norm_gain=key_norm_gain, segment_ids=segment_ids, output_gradient=output_gradient)


EPS = 1e-06

def rms_normalize(inputs, heads, gain_vec):
    as_float = inputs.astype(jnp.float32).reshape(inputs.shape[0], heads, HEAD_SIZE)
    inv_rms = lax.rsqrt(lax.optimization_barrier(jnp.mean(as_float * as_float, -1, keepdims=True)) + EPS)
    normed = as_float * inv_rms
    return (normed, inv_rms, (normed * gain_vec).astype(jnp.bfloat16))

def rms_norm_backward(upstream, normed, inv_rms, gain_vec):
    scaled = upstream * gain_vec
    return inv_rms * (scaled - normed * lax.optimization_barrier(jnp.mean(scaled * normed, -1, keepdims=True)))

def round_down(inputs):
    return lax.optimization_barrier(inputs.astype(jnp.bfloat16))

def one_sequence(q_gain, key_norm_gain, inputs):
    queries, keys, values, segments, output_gradient = inputs
    query_group_width = QUERY_HEADS // KEY_VALUE_HEADS
    score_scale = HEAD_SIZE ** (-0.5)
    window_extent = HALO * DEVICE_TOKENS
    width_all = (HALO + 1) * DEVICE_TOKENS
    q_normed, q_inv, query_norm_result = rms_normalize(queries, QUERY_HEADS, q_gain)
    normalized_keys, key_inverse_rms, key_norm_result = rms_normalize(keys, KEY_VALUE_HEADS, key_norm_gain)
    padded_keys = jnp.concatenate([jnp.zeros((window_extent, KEY_VALUE_HEADS, HEAD_SIZE), jnp.bfloat16), key_norm_result])
    padded_values = jnp.concatenate([jnp.zeros((window_extent, KEY_VALUE_HEADS, HEAD_SIZE), jnp.bfloat16), values.reshape(SEQUENCE_LENGTH, KEY_VALUE_HEADS, HEAD_SIZE)])
    seg_padded = jnp.concatenate([jnp.full((window_extent,), -1, jnp.int32), segments.astype(jnp.int32)])
    offsets = jnp.arange(DEVICE_TOKENS, dtype=jnp.int32)
    key_offsets = jnp.arange(width_all, dtype=jnp.int32)
    distance = offsets[:, None] + window_extent - key_offsets[None, :]
    in_window = (distance >= 0) & (distance < WINDOW)
    gradient_bundle = output_gradient.reshape(SEQUENCE_LENGTH, KEY_VALUE_HEADS, query_group_width, HEAD_SIZE)

    def step(carry, shard):
        key_acc, value_accumulator, gain_acc = carry
        start = (shard * DEVICE_TOKENS).astype(jnp.int32)
        query_block = lax.dynamic_slice_in_dim(query_norm_result, start, DEVICE_TOKENS, 0)
        query_block = query_block.reshape(DEVICE_TOKENS, KEY_VALUE_HEADS, query_group_width, HEAD_SIZE).astype(jnp.float32)
        q_seg = lax.dynamic_slice_in_dim(segments.astype(jnp.int32), start, DEVICE_TOKENS, 0)
        key_block = lax.dynamic_slice_in_dim(padded_keys, start, width_all, 0).astype(jnp.float32)
        value_block = lax.dynamic_slice_in_dim(padded_values, start, width_all, 0).astype(jnp.float32)
        key_seg = lax.dynamic_slice_in_dim(seg_padded, start, width_all, 0)
        key_mask = in_window & (q_seg[:, None] == key_seg[None, :])
        scores = jnp.einsum('qhgd,khd->hgqk', query_block, key_block) * score_scale
        exp_scores = jnp.where(key_mask, jnp.exp(scores), 0.0)
        probs = exp_scores / lax.optimization_barrier(jnp.sum(exp_scores, -1, keepdims=True))
        probs_f = round_down(probs).astype(jnp.float32)
        attn_block = round_down(jnp.einsum('hgqk,khd->qhgd', probs_f, value_block))
        grad_block = lax.dynamic_slice_in_dim(gradient_bundle, start, DEVICE_TOKENS, 0).astype(jnp.float32)
        row_delta = lax.optimization_barrier(jnp.sum(grad_block * attn_block.astype(jnp.float32), -1)).transpose(1, 2, 0)
        prob_grad = jnp.einsum('qhgd,khd->hgqk', grad_block, value_block)
        score_grad = round_down(probs * (prob_grad - row_delta[..., None])).astype(jnp.float32)
        q_grad = jnp.einsum('hgqk,khd->qhgd', score_grad, key_block) * score_scale
        q_grad = q_grad.reshape(DEVICE_TOKENS, QUERY_HEADS, HEAD_SIZE)
        key_term = round_down(jnp.einsum('hgqk,qhgd->khd', score_grad, query_block) * score_scale).astype(jnp.float32)
        value_term = round_down(jnp.einsum('hgqk,qhgd->khd', probs_f, grad_block)).astype(jnp.float32)
        key_now = lax.dynamic_slice_in_dim(key_acc, start, width_all, 0)
        key_acc = lax.dynamic_update_slice_in_dim(key_acc, key_now + key_term, start, 0)
        value_now = lax.dynamic_slice_in_dim(value_accumulator, start, width_all, 0)
        value_accumulator = lax.dynamic_update_slice_in_dim(value_accumulator, value_now + value_term, start, 0)
        normed_block = lax.dynamic_slice_in_dim(q_normed, start, DEVICE_TOKENS, 0)
        inv_block = lax.dynamic_slice_in_dim(q_inv, start, DEVICE_TOKENS, 0)
        dq_block = rms_norm_backward(q_grad, normed_block, inv_block, q_gain).astype(jnp.bfloat16)
        gain_acc = gain_acc + lax.optimization_barrier(jnp.sum(q_grad * normed_block, (0, 1)))
        outputs = (attn_block.reshape(DEVICE_TOKENS, QUERY_HEADS * HEAD_SIZE), dq_block.reshape(DEVICE_TOKENS, QUERY_HEADS * HEAD_SIZE))
        return ((key_acc, value_accumulator, gain_acc), outputs)
    starting_carry = (jnp.zeros((window_extent + SEQUENCE_LENGTH, KEY_VALUE_HEADS, HEAD_SIZE), jnp.float32), jnp.zeros((window_extent + SEQUENCE_LENGTH, KEY_VALUE_HEADS, HEAD_SIZE), jnp.float32), jnp.zeros((HEAD_SIZE,), jnp.float32))
    finals, stacked = lax.scan(step, starting_carry, jnp.arange(N_CTX, dtype=jnp.int32))
    key_acc, value_accumulator, q_sum = finals
    attn_blocks, dq_blocks = stacked
    key_norm_gradient = key_acc[window_extent:]
    key_gradient = rms_norm_backward(key_norm_gradient, normalized_keys, key_inverse_rms, key_norm_gain).astype(jnp.bfloat16).reshape(SEQUENCE_LENGTH, KEY_VALUE_HEADS * HEAD_SIZE)
    value_gradient = value_accumulator[window_extent:].astype(jnp.bfloat16).reshape(SEQUENCE_LENGTH, KEY_VALUE_HEADS * HEAD_SIZE)
    k_sum = lax.optimization_barrier(jnp.sum(key_norm_gradient * normalized_keys, (0, 1)))
    return (attn_blocks.reshape(SEQUENCE_LENGTH, QUERY_HEADS * HEAD_SIZE), dq_blocks.reshape(SEQUENCE_LENGTH, QUERY_HEADS * HEAD_SIZE), key_gradient, value_gradient, q_sum, k_sum)

def reference(queries, keys, values, q_gain, key_norm_gain, segment_ids, output_gradient):
    results = lax.map(partial(one_sequence, q_gain, key_norm_gain), (queries, keys, values, segment_ids, output_gradient))
    attn_out, grad_queries, key_gradient, value_gradient, q_sums, k_sums = results
    factor = (SEQUENCE_LENGTH * SEQUENCE_COUNT) ** (-0.5)
    return (attn_out, grad_queries, key_gradient, value_gradient, lax.optimization_barrier(jnp.sum(q_sums, 0)) * factor, lax.optimization_barrier(jnp.sum(k_sums, 0)) * factor)
```

```python
import functools

import jax
import jax.numpy as jnp
from jax import lax
from jax.experimental import pallas as pl
from jax.experimental.pallas import tpu as pltpu
from jax.sharding import PartitionSpec as P

HEADS = 8
KV = 4
D = 256
WINDOW = 256
HALO = 2
EPS = 1e-06
SCALE = D ** (-0.5)
MESH = pl.DeviceIdType.MESH
F32 = jnp.float32
BF16 = jnp.bfloat16


def dot(a, b, contract):
    return lax.dot_general(a, b, ((contract[:1], contract[1:]), ((), ())), preferred_element_type=F32)


def hat(x):
    x = x.astype(F32)
    inv = lax.rsqrt(jnp.mean(x * x, -1, keepdims=True) + EPS)
    return x * inv, inv


def norm_backward(up, normed, inv, gain):
    g = up * gain
    return inv * (g - normed * jnp.mean(g * normed, -1, keepdims=True))


def kernel(
    nc, nd,
    q_ref, k_ref, v_ref, qg_ref, kg_ref, seg_ref, do_ref,
    o_ref, dq_ref, dk_ref, dv_ref, gq_ref, gk_ref,
    kvbuf, segbuf, gbuf, grecv, own, part_c, part_d, stage_c, stage_d,
    kv_send, kv_recv, seg_send, seg_recv, g_send, g_recv, r_send, r_recv,
):
    T = k_ref.shape[1]
    me = lax.axis_index("ctx")
    dpi = lax.axis_index("dp")

    barrier = pltpu.get_barrier_semaphore()

    @pl.loop(1, nc)
    def _(d):
        pl.semaphore_signal(barrier, inc=1, device_id={"ctx": lax.rem(me + d, nc)}, device_id_type=MESH)

    @pl.loop(1, nd)
    def _(d):
        pl.semaphore_signal(barrier, inc=1, device_id={"dp": lax.rem(dpi + d, nd)}, device_id_type=MESH)

    def remote(src, dst, send, recv, peer):
        return pltpu.make_async_remote_copy(
            src_ref=src, dst_ref=dst, send_sem=send, recv_sem=recv,
            device_id=peer, device_id_type=MESH,
        )

    def rows(block):
        return pl.ds(block * T, T)

    def kv_copy(g, off):
        return remote(
            kvbuf.at[g, rows(HALO)], kvbuf.at[g, rows(HALO - off)],
            kv_send.at[off - 1, g], kv_recv.at[off - 1, g], {"ctx": me + off},
        )

    def seg_copy(off):
        return remote(
            segbuf.at[HALO], segbuf.at[HALO - off],
            seg_send.at[off - 1], seg_recv.at[off - 1], {"ctx": me + off},
        )

    def grad_copy(g, off):
        return remote(
            gbuf.at[g, rows(HALO - off)], grecv.at[off - 1, g],
            g_send.at[off - 1, g], g_recv.at[off - 1, g], {"ctx": me - off},
        )

    q_gain = qg_ref[...]
    k_gain = kg_ref[...]
    for g in range(KV):
        col = pl.ds(g * D, D)
        kvbuf[g, rows(HALO), 0:D] = (hat(k_ref[0, :, col])[0] * k_gain).astype(BF16)
        kvbuf[g, rows(HALO), D:] = v_ref[0, :, col]
    seg_row = seg_ref[...]
    segbuf[HALO] = jnp.broadcast_to(seg_row, (8, T))

    pl.semaphore_wait(barrier, nc - 1 + nd - 1)

    for off in range(1, HALO + 1):
        @pl.when(me + off < nc)
        def _(off=off):
            seg_copy(off).start()

    for g in range(KV):
        for off in range(1, HALO + 1):
            @pl.when(me + off < nc)
            def _(off=off, g=g):
                kv_copy(g, off).start()

    for off in range(1, HALO + 1):
        @pl.when(me < off)
        def _(off=off):
            for g in range(KV):
                kvbuf[g, rows(HALO - off)] = jnp.zeros((T, 2 * D), BF16)
            segbuf[HALO - off] = jnp.full((8, T), -1, jnp.int32)

        @pl.when(me + off >= nc)
        def _(off=off):
            for g in range(KV):
                grecv[off - 1, g] = jnp.zeros((T, 2 * D), BF16)

    qs = []
    for h in range(HEADS):
        q_hat, _ = hat(q_ref[0, :, pl.ds(h * D, D)])
        qs.append((q_hat * q_gain).astype(BF16) * jnp.asarray(SCALE, BF16))

    seg_q = jnp.broadcast_to(seg_row, (T, T)).T
    for off in range(1, HALO + 1):
        @pl.when(me >= off)
        def _(off=off):
            seg_copy(off).wait_recv()
    qi = lax.broadcasted_iota(jnp.int32, (T, T), 0)
    ki = lax.broadcasted_iota(jnp.int32, (T, T), 1)
    masks = []
    for block in range(HALO + 1):
        dist = qi - ki + (HALO - block) * T
        same = seg_q == jnp.broadcast_to(segbuf[block, 0:1, :], (T, T))
        masks.append((dist >= 0) & (dist < WINDOW) & same)
    mask = jnp.concatenate(masks, 1)
    mask = jnp.concatenate([mask, mask], 0)

    gq = jnp.zeros((1, D), F32)
    gk = jnp.zeros((1, D), F32)
    for g in range(KV):
        for off in range(1, HALO + 1):
            @pl.when(me >= off)
            def _(off=off, g=g):
                kv_copy(g, off).wait_recv()
        K = kvbuf[g, :, 0:D]
        V = kvbuf[g, :, D:]
        Q = jnp.concatenate([qs[2 * g], qs[2 * g + 1]], 0)
        dO = jnp.concatenate(
            [do_ref[0, :, pl.ds(2 * g * D, D)], do_ref[0, :, pl.ds((2 * g + 1) * D, D)]], 0
        )
        E = jnp.where(mask, jnp.exp(dot(Q, K, (1, 1))), 0.0)
        prob = E * (1.0 / jnp.sum(E, -1, keepdims=True))
        prob_b = prob.astype(BF16)
        out = dot(prob_b, V, (1, 0)).astype(BF16)
        for i in range(2):
            o_ref[0, :, pl.ds((2 * g + i) * D, D)] = out[i * T:(i + 1) * T]
        delta = jnp.sum(dO.astype(F32) * out.astype(F32), -1, keepdims=True)
        ds = (prob * (dot(dO, V, (1, 1)) - delta)).astype(BF16)
        dK = dot(ds, Q, (0, 0))
        dV = dot(prob_b, dO, (0, 0))
        gbuf[g, :, 0:D] = dK[:HALO * T].astype(BF16)
        gbuf[g, :, D:] = dV[:HALO * T].astype(BF16)
        for off in range(1, HALO + 1):
            @pl.when(me >= off)
            def _(off=off, g=g):
                grad_copy(g, off).start()
        own[g, :, 0:D] = dK[HALO * T:]
        own[g, :, D:] = dV[HALO * T:]
        gk += jnp.sum(dK * K.astype(F32), 0, keepdims=True)
        dQ = dot(ds, K, (1, 0)) * SCALE
        for i in range(2):
            col = pl.ds((2 * g + i) * D, D)
            q_hat, q_inv = hat(q_ref[0, :, col])
            up = dQ[i * T:(i + 1) * T]
            gq += jnp.sum(up * q_hat, 0, keepdims=True)
            dq_ref[0, :, col] = norm_backward(up, q_hat, q_inv, q_gain).astype(BF16)

    def reduce_over(axis, count, index, part, stage, which):
        def one(d):
            return remote(
                part, stage.at[d - 1], r_send.at[which], r_recv.at[which],
                {axis: lax.rem(index + d, count)},
            )

        @pl.loop(1, count)
        def _(d):
            one(d).start()

        pltpu.make_async_copy(stage, stage, r_recv.at[which]).wait()
        return part[...] + jnp.sum(stage[...], 0)

    part_c[0:1, :] = gq
    part_c[1:2, :] = gk / k_gain
    part_d[...] = reduce_over("ctx", nc, me, part_c, stage_c, 0)
    total = reduce_over("dp", nd, dpi, part_d, stage_d, 1) * float(nc * nd * T) ** (-0.5)
    gq_ref[...] = total[0:1]
    gk_ref[...] = total[1:2]

    for g in range(KV):
        for off in range(1, HALO + 1):
            @pl.when(me + off < nc)
            def _(off=off, g=g):
                grad_copy(g, off).wait_recv()
        col = pl.ds(g * D, D)
        acc = own[g] + grecv[0, g].astype(F32) + grecv[1, g].astype(F32)
        k_hat, k_inv = hat(k_ref[0, :, col])
        dk_ref[0, :, col] = norm_backward(acc[:, 0:D], k_hat, k_inv, k_gain).astype(BF16)
        dv_ref[0, :, col] = acc[:, D:].astype(BF16)

    for off in range(1, HALO + 1):
        @pl.when(me + off < nc)
        def _(off=off):
            seg_copy(off).wait_send()
            for g in range(KV):
                kv_copy(g, off).wait_send()

        @pl.when(me >= off)
        def _(off=off):
            for g in range(KV):
                grad_copy(g, off).wait_send()
    pltpu.make_async_copy(stage_c, stage_c, r_send.at[0]).wait()
    pltpu.make_async_copy(stage_d, stage_d, r_send.at[1]).wait()


def body(nc, nd, queries, keys, values, q_gain, key_norm_gain, segment_ids, output_gradient):
    T = queries.shape[1]
    dma = pltpu.SemaphoreType.DMA
    vmem = pl.BlockSpec(memory_space=pltpu.VMEM)
    outs = pl.pallas_call(
        functools.partial(kernel, nc, nd),
        out_shape=(
            jax.ShapeDtypeStruct(queries.shape, BF16),
            jax.ShapeDtypeStruct(queries.shape, BF16),
            jax.ShapeDtypeStruct(keys.shape, BF16),
            jax.ShapeDtypeStruct(values.shape, BF16),
            jax.ShapeDtypeStruct((1, D), F32),
            jax.ShapeDtypeStruct((1, D), F32),
        ),
        in_specs=[vmem] * 7,
        out_specs=(vmem,) * 6,
        scratch_shapes=[
            pltpu.VMEM((KV, (HALO + 1) * T, 2 * D), BF16),
            pltpu.VMEM((HALO + 1, 8, T), jnp.int32),
            pltpu.VMEM((KV, HALO * T, 2 * D), BF16),
            pltpu.VMEM((HALO, KV, T, 2 * D), BF16),
            pltpu.VMEM((KV, T, 2 * D), F32),
            pltpu.VMEM((2, D), F32),
            pltpu.VMEM((2, D), F32),
            pltpu.VMEM((nc - 1, 2, D), F32),
            pltpu.VMEM((nd - 1, 2, D), F32),
            dma((HALO, KV)), dma((HALO, KV)),
            dma((HALO,)), dma((HALO,)),
            dma((HALO, KV)), dma((HALO, KV)),
            dma((2,)), dma((2,)),
        ],
        compiler_params=pltpu.CompilerParams(
            collective_id=0, has_side_effects=True, vmem_limit_bytes=48 * 1024 * 1024,
        ),
    )(queries, keys, values, q_gain.reshape(1, D), key_norm_gain.reshape(1, D), segment_ids, output_gradient)
    attn_out, dq, dk, dv, gq, gk = outs
    return attn_out, dq, dk, dv, gq.reshape(D), gk.reshape(D)


def solution(mesh):
    tokens = P("dp", "ctx", None)
    return jax.shard_map(
        functools.partial(body, mesh.shape["ctx"], mesh.shape["dp"]),
        mesh=mesh,
        in_specs=(tokens, tokens, tokens, P(), P(), P("dp", "ctx"), tokens),
        out_specs=(tokens, tokens, tokens, tokens, P(), P()),
        check_vma=False,
    )
```

```python
import functools

import jax
import jax.numpy as jnp
from jax import lax
from jax.experimental import pallas as pl
from jax.experimental.pallas import tpu as pltpu
from jax.sharding import PartitionSpec as P

HEADS = 8
KV = 4
D = 256
WINDOW = 256
HALO = 2
EPS = 1e-06
SCALE = D ** (-0.5)
MESH = pl.DeviceIdType.MESH
F32 = jnp.float32
BF16 = jnp.bfloat16


def dot(a, b, contract):
    return lax.dot_general(a, b, ((contract[:1], contract[1:]), ((), ())), preferred_element_type=F32)


def hat(x):
    x = x.astype(F32)
    inv = lax.rsqrt(jnp.mean(x * x, -1, keepdims=True) + EPS)
    return x * inv, inv


def norm_backward(up, normed, inv, gain):
    g = up * gain
    return inv * (g - normed * jnp.mean(g * normed, -1, keepdims=True))


def kernel(
    nc, nd,
    q_hbm, k_hbm, v_hbm, qg_hbm, kg_hbm, seg_hbm, do_hbm,
    o_hbm, dq_hbm, dk_hbm, dv_hbm, gq_hbm, gk_hbm,
    q_ref, k_ref, do_ref, qg_ref, kg_ref, seg_ref, in_sem,
    o_ref, dq_ref, dk_ref, dv_ref, gq_ref, gk_ref, out_sem, gain_sem,
    kvbuf, segbuf, gbuf, grecv, own, part, stage,
    kv_send, kv_recv, seg_send, seg_recv, g_send, g_recv, r_send, r_recv,
):
    T = k_hbm.shape[1]
    me = lax.axis_index("ctx")
    dpi = lax.axis_index("dp")

    loads = {}

    def load(name, src, dst):
        loads[name] = pltpu.make_async_copy(src, dst, in_sem.at[len(loads)])
        loads[name].start()

    stores = []

    def store(src, dst, sem):
        stores.append(pltpu.make_async_copy(src, dst, sem))
        stores[-1].start()

    def arrive(name):
        loads[name].wait()

    load("kg", kg_hbm, kg_ref)
    for g in range(KV):
        col = pl.ds(g * D, D)
        load(f"k{g}", k_hbm.at[0, :, col], k_ref.at[:, col])
        load(f"v{g}", v_hbm.at[0, :, col], kvbuf.at[g, pl.ds(HALO * T, T), pl.ds(D, D)])
    load("seg", seg_hbm, seg_ref)
    load("qg", qg_hbm, qg_ref)
    load("q", q_hbm.at[0], q_ref)
    load("do", do_hbm.at[0], do_ref)

    barrier = pltpu.get_barrier_semaphore()

    rank = me * nd + dpi

    def peer_of(d):
        other = lax.rem(rank + d, nc * nd)
        return {"ctx": other // nd, "dp": lax.rem(other, nd)}

    @pl.loop(1, nc * nd)
    def _(d):
        pl.semaphore_signal(barrier, inc=1, device_id=peer_of(d), device_id_type=MESH)

    def remote(src, dst, send, recv, peer):
        return pltpu.make_async_remote_copy(
            src_ref=src, dst_ref=dst, send_sem=send, recv_sem=recv,
            device_id=peer, device_id_type=MESH,
        )

    def rows(block):
        return pl.ds(block * T, T)

    def kv_copy(g, off):
        return remote(
            kvbuf.at[g, rows(HALO)], kvbuf.at[g, rows(HALO - off)],
            kv_send.at[off - 1, g], kv_recv.at[off - 1, g], {"ctx": me + off},
        )

    def seg_copy(off):
        return remote(
            segbuf.at[HALO], segbuf.at[HALO - off],
            seg_send.at[off - 1], seg_recv.at[off - 1], {"ctx": me + off},
        )

    def sum_copy(d):
        return remote(part, stage.at[d - 1], r_send, r_recv, peer_of(d))

    def grad_copy(g, off):
        return remote(
            gbuf.at[g, rows(HALO - off)], grecv.at[off - 1, g],
            g_send.at[off - 1, g], g_recv.at[off - 1, g], {"ctx": me - off},
        )

    arrive("kg")
    k_gain = kg_ref[...]
    for g in range(KV):
        col = pl.ds(g * D, D)
        arrive(f"k{g}")
        kvbuf[g, rows(HALO), 0:D] = (hat(k_ref[:, col])[0] * k_gain).astype(BF16)
        arrive(f"v{g}")
        if g == 0:
            arrive("seg")
            seg_row = seg_ref[...]
            segbuf[HALO] = jnp.broadcast_to(seg_row, (8, T))
            pl.semaphore_wait(barrier, nc * nd - 1)
            for off in range(1, HALO + 1):
                @pl.when(me + off < nc)
                def _(off=off):
                    seg_copy(off).start()
        for off in range(1, HALO + 1):
            @pl.when(me + off < nc)
            def _(off=off, g=g):
                kv_copy(g, off).start()

    for off in range(1, HALO + 1):
        @pl.when(me < off)
        def _(off=off):
            for g in range(KV):
                kvbuf[g, rows(HALO - off)] = jnp.zeros((T, 2 * D), BF16)
            segbuf[HALO - off] = jnp.full((8, T), -1, jnp.int32)

        @pl.when(me + off >= nc)
        def _(off=off):
            for g in range(KV):
                grecv[off - 1, g] = jnp.zeros((T, 2 * D), BF16)

    arrive("qg")
    q_gain = qg_ref[...]
    arrive("q")
    qs = []
    for h in range(HEADS):
        q_hat, _ = hat(q_ref[:, pl.ds(h * D, D)])
        qs.append((q_hat * q_gain).astype(BF16) * jnp.asarray(SCALE, BF16))

    seg_q = jnp.broadcast_to(seg_row, (T, T)).T
    for off in range(1, HALO + 1):
        @pl.when(me >= off)
        def _(off=off):
            seg_copy(off).wait_recv()
    qi = lax.broadcasted_iota(jnp.int32, (T, T), 0)
    ki = lax.broadcasted_iota(jnp.int32, (T, T), 1)
    masks = []
    for block in range(HALO + 1):
        dist = qi - ki + (HALO - block) * T
        same = seg_q == jnp.broadcast_to(segbuf[block, 0:1, :], (T, T))
        masks.append((dist >= 0) & (dist < WINDOW) & same)
    mask = jnp.concatenate(masks, 1)
    mask = jnp.concatenate([mask, mask], 0)

    arrive("do")
    gq = jnp.zeros((1, D), F32)
    gk = jnp.zeros((1, D), F32)
    for g in range(KV):
        for off in range(1, HALO + 1):
            @pl.when(me >= off)
            def _(off=off, g=g):
                kv_copy(g, off).wait_recv()
        K = kvbuf[g, :, 0:D]
        V = kvbuf[g, :, D:]
        Q = jnp.concatenate([qs[2 * g], qs[2 * g + 1]], 0)
        dO = jnp.concatenate(
            [do_ref[:, pl.ds(2 * g * D, D)], do_ref[:, pl.ds((2 * g + 1) * D, D)]], 0
        )
        E = jnp.where(mask, jnp.exp(dot(Q, K, (1, 1))), 0.0)
        prob = E * (1.0 / jnp.sum(E, -1, keepdims=True))
        prob_b = prob.astype(BF16)
        out = dot(prob_b, V, (1, 0)).astype(BF16)
        for i in range(2):
            o_ref[:, pl.ds((2 * g + i) * D, D)] = out[i * T:(i + 1) * T]
        delta = jnp.sum(dO.astype(F32) * out.astype(F32), -1, keepdims=True)
        ds = (prob * (dot(dO, V, (1, 1)) - delta)).astype(BF16)
        dK = dot(ds, Q, (0, 0))
        dV = dot(prob_b, dO, (0, 0))
        gbuf[g, :, 0:D] = dK[:HALO * T].astype(BF16)
        gbuf[g, :, D:] = dV[:HALO * T].astype(BF16)
        for off in range(1, HALO + 1):
            @pl.when(me >= off)
            def _(off=off, g=g):
                grad_copy(g, off).start()
        own[g, :, 0:D] = dK[HALO * T:]
        own[g, :, D:] = dV[HALO * T:]
        gk += jnp.sum(dK * K.astype(F32), 0, keepdims=True)
        dQ = dot(ds, K, (1, 0)) * SCALE
        for i in range(2):
            col = pl.ds((2 * g + i) * D, D)
            q_hat, q_inv = hat(q_ref[:, col])
            up = dQ[i * T:(i + 1) * T]
            gq += jnp.sum(up * q_hat, 0, keepdims=True)
            dq_ref[:, col] = norm_backward(up, q_hat, q_inv, q_gain).astype(BF16)
        pair = pl.ds(2 * g * D, 2 * D)
        store(o_ref.at[:, pair], o_hbm.at[0, :, pair], out_sem.at[0, g])
        store(dq_ref.at[:, pair], dq_hbm.at[0, :, pair], out_sem.at[1, g])

    part[0:1, :] = gq
    part[1:2, :] = gk / k_gain

    @pl.loop(1, nc * nd)
    def _(d):
        sum_copy(d).start()

    for g in range(KV):
        for off in range(1, HALO + 1):
            @pl.when(me + off < nc)
            def _(off=off, g=g):
                grad_copy(g, off).wait_recv()
        col = pl.ds(g * D, D)
        acc = own[g] + grecv[0, g].astype(F32) + grecv[1, g].astype(F32)
        k_hat, k_inv = hat(k_ref[:, col])
        dk_ref[:, col] = norm_backward(acc[:, 0:D], k_hat, k_inv, k_gain).astype(BF16)
        dv_ref[:, col] = acc[:, D:].astype(BF16)
        store(dk_ref.at[:, col], dk_hbm.at[0, :, col], out_sem.at[2, g])
        store(dv_ref.at[:, col], dv_hbm.at[0, :, col], out_sem.at[3, g])

    for off in range(1, HALO + 1):
        @pl.when(me + off < nc)
        def _(off=off):
            seg_copy(off).wait_send()
            for g in range(KV):
                kv_copy(g, off).wait_send()

        @pl.when(me >= off)
        def _(off=off):
            for g in range(KV):
                grad_copy(g, off).wait_send()
    pltpu.make_async_copy(stage, stage, r_send).wait()
    pltpu.make_async_copy(stage, stage, r_recv).wait()
    total = (part[...] + jnp.sum(stage[...], 0)) * float(nc * nd * T) ** (-0.5)
    gq_ref[...] = total[0:1]
    gk_ref[...] = total[1:2]
    store(gq_ref, gq_hbm, gain_sem.at[0])
    store(gk_ref, gk_hbm, gain_sem.at[1])
    for copy in stores:
        copy.wait()


def deliver_kernel(*refs):
    n = len(refs) // 2
    sems = refs[-1]
    copies = [pltpu.make_async_copy(refs[i], refs[n + i], sems.at[i]) for i in range(n)]
    for copy in copies:
        copy.start()
    for copy in copies:
        copy.wait()


def deliver(*arrays):
    return pl.pallas_call(
        deliver_kernel,
        out_shape=tuple(jax.ShapeDtypeStruct(a.shape, a.dtype) for a in arrays),
        in_specs=[pl.BlockSpec(memory_space=pl.ANY)] * len(arrays),
        out_specs=(pl.BlockSpec(memory_space=pl.ANY),) * len(arrays),
        scratch_shapes=[pltpu.SemaphoreType.DMA((len(arrays),))],
    )(*arrays)


def body(nc, nd, queries, keys, values, q_gain, key_norm_gain, segment_ids, output_gradient):
    T = queries.shape[1]
    dma = pltpu.SemaphoreType.DMA
    outs = pl.pallas_call(
        functools.partial(kernel, nc, nd),
        out_shape=(
            jax.ShapeDtypeStruct(queries.shape, BF16),
            jax.ShapeDtypeStruct(queries.shape, BF16),
            jax.ShapeDtypeStruct(keys.shape, BF16),
            jax.ShapeDtypeStruct(values.shape, BF16),
            jax.ShapeDtypeStruct((1, D), F32),
            jax.ShapeDtypeStruct((1, D), F32),
        ),
        in_specs=[pl.BlockSpec(memory_space=pl.ANY)] * 7,
        out_specs=(pl.BlockSpec(memory_space=pl.ANY),) * 6,
        scratch_shapes=[
            pltpu.VMEM((T, HEADS * D), BF16),
            pltpu.VMEM((T, KV * D), BF16),
            pltpu.VMEM((T, HEADS * D), BF16),
            pltpu.VMEM((1, D), F32),
            pltpu.VMEM((1, D), F32),
            pltpu.VMEM((1, T), jnp.int32),
            dma((2 * KV + 5,)),
            pltpu.VMEM((T, HEADS * D), BF16),
            pltpu.VMEM((T, HEADS * D), BF16),
            pltpu.VMEM((T, KV * D), BF16),
            pltpu.VMEM((T, KV * D), BF16),
            pltpu.VMEM((1, D), F32),
            pltpu.VMEM((1, D), F32),
            dma((4, KV)), dma((2,)),
            pltpu.VMEM((KV, (HALO + 1) * T, 2 * D), BF16),
            pltpu.VMEM((HALO + 1, 8, T), jnp.int32),
            pltpu.VMEM((KV, HALO * T, 2 * D), BF16),
            pltpu.VMEM((HALO, KV, T, 2 * D), BF16),
            pltpu.VMEM((KV, T, 2 * D), F32),
            pltpu.VMEM((2, D), F32),
            pltpu.VMEM((nc * nd - 1, 2, D), F32),
            dma((HALO, KV)), dma((HALO, KV)),
            dma((HALO,)), dma((HALO,)),
            dma((HALO, KV)), dma((HALO, KV)),
            dma, dma,
        ],
        compiler_params=pltpu.CompilerParams(
            collective_id=0, has_side_effects=True, vmem_limit_bytes=63 * 1024 * 1024,
        ),
    )(queries, keys, values, q_gain.reshape(1, D), key_norm_gain.reshape(1, D), segment_ids, output_gradient)
    attn_out, dq, dk, dv, gq, gk = deliver(*outs)
    return attn_out, dq, dk, dv, gq.reshape(D), gk.reshape(D)


def solution(mesh):
    tokens = P("dp", "ctx", None)
    return jax.shard_map(
        functools.partial(body, mesh.shape["ctx"], mesh.shape["dp"]),
        mesh=mesh,
        in_specs=(tokens, tokens, tokens, P(), P(), P("dp", "ctx"), tokens),
        out_specs=(tokens, tokens, tokens, tokens, P(), P()),
        check_vma=False,
    )
```

```python
import functools

import jax
import jax.numpy as jnp
from jax import lax
from jax.experimental import pallas as pl
from jax.experimental.pallas import tpu as pltpu
from jax.sharding import PartitionSpec as P

HEADS = 8
KV = 4
D = 256
WINDOW = 256
HALO = 2
EPS = 1e-06
SCALE = D ** (-0.5)
MESH = pl.DeviceIdType.MESH
F32 = jnp.float32
BF16 = jnp.bfloat16


def dot(a, b, contract):
    return lax.dot_general(a, b, ((contract[:1], contract[1:]), ((), ())), preferred_element_type=F32)


def hat(x):
    x = x.astype(F32)
    inv = lax.rsqrt(jnp.mean(x * x, -1, keepdims=True) + EPS)
    return x * inv, inv


def norm_backward(up, normed, inv, gain):
    g = up * gain
    return inv * (g - normed * jnp.mean(g * normed, -1, keepdims=True))


def kernel(
    nc, nd,
    q_hbm, k_hbm, v_hbm, qg_hbm, kg_hbm, seg_hbm, do_hbm,
    o_hbm, dq_hbm, dk_hbm, dv_hbm, gq_hbm, gk_hbm,
    q_ref, k_ref, do_ref, qg_ref, kg_ref, seg_ref, in_sem,
    o_ref, dq_ref, dk_ref, dv_ref, gq_ref, gk_ref, out_sem, gain_sem,
    kvbuf, segbuf, gbuf, grecv, own, part, stage,
    kv_send, kv_recv, seg_send, seg_recv, g_send, g_recv, r_send, r_recv,
):
    T = k_hbm.shape[1]
    me = lax.axis_index("ctx")
    dpi = lax.axis_index("dp")

    loads = {}

    def load(name, src, dst):
        loads[name] = pltpu.make_async_copy(src, dst, in_sem.at[len(loads)])
        loads[name].start()

    stores = []

    def store(src, dst, sem):
        stores.append(pltpu.make_async_copy(src, dst, sem))
        stores[-1].start()

    def arrive(name):
        loads[name].wait()

    load("kg", kg_hbm, kg_ref)
    for g in range(KV):
        col = pl.ds(g * D, D)
        load(f"k{g}", k_hbm.at[0, :, col], k_ref.at[:, col])
        load(f"v{g}", v_hbm.at[0, :, col], kvbuf.at[g, pl.ds(HALO * T, T), pl.ds(D, D)])
    load("seg", seg_hbm, seg_ref)
    load("qg", qg_hbm, qg_ref)
    load("q", q_hbm.at[0], q_ref)
    load("do", do_hbm.at[0], do_ref)

    barrier = pltpu.get_barrier_semaphore()

    rank = me * nd + dpi

    def peer_of(d):
        other = lax.rem(rank + d, nc * nd)
        return {"ctx": other // nd, "dp": lax.rem(other, nd)}

    @pl.loop(1, nc * nd)
    def _(d):
        pl.semaphore_signal(barrier, inc=1, device_id=peer_of(d), device_id_type=MESH)

    def remote(src, dst, send, recv, peer):
        return pltpu.make_async_remote_copy(
            src_ref=src, dst_ref=dst, send_sem=send, recv_sem=recv,
            device_id=peer, device_id_type=MESH,
        )

    def rows(block):
        return pl.ds(block * T, T)

    def kv_copy(g, off):
        return remote(
            kvbuf.at[g, rows(HALO)], kvbuf.at[g, rows(HALO - off)],
            kv_send.at[off - 1, g], kv_recv.at[off - 1, g], {"ctx": me + off},
        )

    def seg_copy(off):
        return remote(
            segbuf.at[HALO], segbuf.at[HALO - off],
            seg_send.at[off - 1], seg_recv.at[off - 1], {"ctx": me + off},
        )

    def sum_copy(d):
        return remote(part, stage.at[d - 1], r_send, r_recv, peer_of(d))

    def grad_copy(g, off):
        return remote(
            gbuf.at[g, rows(HALO - off)], grecv.at[off - 1, g],
            g_send.at[off - 1, g], g_recv.at[off - 1, g], {"ctx": me - off},
        )

    arrive("kg")
    k_gain = kg_ref[...]
    for g in range(KV):
        col = pl.ds(g * D, D)
        arrive(f"k{g}")
        kvbuf[g, rows(HALO), 0:D] = (hat(k_ref[:, col])[0] * k_gain).astype(BF16)
        arrive(f"v{g}")
        if g == 0:
            arrive("seg")
            seg_row = seg_ref[...]
            segbuf[HALO] = jnp.broadcast_to(seg_row, (8, T))
            pl.semaphore_wait(barrier, nc * nd - 1)
            for off in range(1, HALO + 1):
                @pl.when(me + off < nc)
                def _(off=off):
                    seg_copy(off).start()
        for off in range(1, HALO + 1):
            @pl.when(me + off < nc)
            def _(off=off, g=g):
                kv_copy(g, off).start()

    for off in range(1, HALO + 1):
        @pl.when(me < off)
        def _(off=off):
            for g in range(KV):
                kvbuf[g, rows(HALO - off)] = jnp.zeros((T, 2 * D), BF16)
            segbuf[HALO - off] = jnp.full((8, T), -1, jnp.int32)

        @pl.when(me + off >= nc)
        def _(off=off):
            for g in range(KV):
                grecv[off - 1, g] = jnp.zeros((T, 2 * D), BF16)

    arrive("qg")
    q_gain = qg_ref[...]
    arrive("q")
    qs = []
    for h in range(HEADS):
        q_hat, _ = hat(q_ref[:, pl.ds(h * D, D)])
        qs.append((q_hat * q_gain).astype(BF16) * jnp.asarray(SCALE, BF16))

    seg_q = jnp.broadcast_to(seg_row, (T, T)).T
    for off in range(1, HALO + 1):
        @pl.when(me >= off)
        def _(off=off):
            seg_copy(off).wait_recv()
    qi = lax.broadcasted_iota(jnp.int32, (T, T), 0)
    ki = lax.broadcasted_iota(jnp.int32, (T, T), 1)
    masks = []
    for block in range(HALO + 1):
        dist = qi - ki + (HALO - block) * T
        same = seg_q == jnp.broadcast_to(segbuf[block, 0:1, :], (T, T))
        masks.append((dist >= 0) & (dist < WINDOW) & same)
    mask = jnp.concatenate(masks, 1)
    mask = jnp.concatenate([mask, mask], 0)

    arrive("do")
    gq = jnp.zeros((1, D), F32)
    gk = jnp.zeros((1, D), F32)
    for g in range(KV):
        for off in range(1, HALO + 1):
            @pl.when(me >= off)
            def _(off=off, g=g):
                kv_copy(g, off).wait_recv()
        K = kvbuf[g, :, 0:D]
        V = kvbuf[g, :, D:]
        Q = jnp.concatenate([qs[2 * g], qs[2 * g + 1]], 0)
        dO = jnp.concatenate(
            [do_ref[:, pl.ds(2 * g * D, D)], do_ref[:, pl.ds((2 * g + 1) * D, D)]], 0
        )
        E = jnp.where(mask, jnp.exp(dot(Q, K, (1, 1))), 0.0)
        prob = E * (1.0 / jnp.sum(E, -1, keepdims=True))
        prob_b = prob.astype(BF16)
        out = dot(prob_b, V, (1, 0)).astype(BF16)
        for i in range(2):
            o_ref[:, pl.ds((2 * g + i) * D, D)] = out[i * T:(i + 1) * T]
        delta = jnp.sum(dO.astype(F32) * out.astype(F32), -1, keepdims=True)
        ds = (prob * (dot(dO, V, (1, 1)) - delta)).astype(BF16)
        dK = dot(ds, Q, (0, 0))
        dV = dot(prob_b, dO, (0, 0))
        gbuf[g, :, 0:D] = dK[:HALO * T].astype(BF16)
        gbuf[g, :, D:] = dV[:HALO * T].astype(BF16)
        for off in range(1, HALO + 1):
            @pl.when(me >= off)
            def _(off=off, g=g):
                grad_copy(g, off).start()
        own[g, :, 0:D] = dK[HALO * T:]
        own[g, :, D:] = dV[HALO * T:]
        gk += jnp.sum(dK * K.astype(F32), 0, keepdims=True)
        dQ = dot(ds, K, (1, 0)) * SCALE
        for i in range(2):
            col = pl.ds((2 * g + i) * D, D)
            q_hat, q_inv = hat(q_ref[:, col])
            up = dQ[i * T:(i + 1) * T]
            gq += jnp.sum(up * q_hat, 0, keepdims=True)
            dq_ref[:, col] = norm_backward(up, q_hat, q_inv, q_gain).astype(BF16)
        pair = pl.ds(2 * g * D, 2 * D)
        store(o_ref.at[:, pair], o_hbm.at[0, :, pair], out_sem.at[0, g])
        store(dq_ref.at[:, pair], dq_hbm.at[0, :, pair], out_sem.at[1, g])

    part[0:1, :] = gq
    part[1:2, :] = gk / k_gain

    @pl.loop(1, nc * nd)
    def _(d):
        sum_copy(d).start()

    for g in range(KV):
        for off in range(1, HALO + 1):
            @pl.when(me + off < nc)
            def _(off=off, g=g):
                grad_copy(g, off).wait_recv()
        col = pl.ds(g * D, D)
        acc = own[g] + grecv[0, g].astype(F32) + grecv[1, g].astype(F32)
        k_hat, k_inv = hat(k_ref[:, col])
        dk_ref[:, col] = norm_backward(acc[:, 0:D], k_hat, k_inv, k_gain).astype(BF16)
        dv_ref[:, col] = acc[:, D:].astype(BF16)
        store(dk_ref.at[:, col], dk_hbm.at[0, :, col], out_sem.at[2, g])
        store(dv_ref.at[:, col], dv_hbm.at[0, :, col], out_sem.at[3, g])

    for off in range(1, HALO + 1):
        @pl.when(me + off < nc)
        def _(off=off):
            seg_copy(off).wait_send()
            for g in range(KV):
                kv_copy(g, off).wait_send()

        @pl.when(me >= off)
        def _(off=off):
            for g in range(KV):
                grad_copy(g, off).wait_send()
    pltpu.make_async_copy(stage, stage, r_send).wait()
    pltpu.make_async_copy(stage, stage, r_recv).wait()
    total = (part[...] + jnp.sum(stage[...], 0)) * float(nc * nd * T) ** (-0.5)
    gq_ref[...] = total[0:1]
    gk_ref[...] = total[1:2]
    store(gq_ref, gq_hbm, gain_sem.at[0])
    store(gk_ref, gk_hbm, gain_sem.at[1])
    for copy in stores:
        copy.wait()


def deliver_kernel(*refs):
    n = (len(refs) - 2) // 3
    ins, outs, held = refs[:n], refs[n:2 * n], refs[2 * n:3 * n]
    in_sem, out_sem = refs[-2:]
    loads = [pltpu.make_async_copy(ins[i], held[i], in_sem.at[i]) for i in range(n)]
    stores = [pltpu.make_async_copy(held[i], outs[i], out_sem.at[i]) for i in range(n)]
    for copy in loads:
        copy.start()
    for i in range(n):
        loads[i].wait()
        stores[i].start()
    for copy in stores:
        copy.wait()


def deliver(*arrays):
    n = len(arrays)
    anywhere = pl.BlockSpec(memory_space=pl.ANY)
    return pl.pallas_call(
        deliver_kernel,
        out_shape=tuple(jax.ShapeDtypeStruct(a.shape, a.dtype) for a in arrays),
        in_specs=[anywhere] * n,
        out_specs=(anywhere,) * n,
        scratch_shapes=[pltpu.VMEM(a.shape, a.dtype) for a in arrays]
        + [pltpu.SemaphoreType.DMA((n,))] * 2,
        compiler_params=pltpu.CompilerParams(vmem_limit_bytes=63 * 1024 * 1024),
    )(*arrays)


def body(nc, nd, queries, keys, values, q_gain, key_norm_gain, segment_ids, output_gradient):
    T = queries.shape[1]
    dma = pltpu.SemaphoreType.DMA
    outs = pl.pallas_call(
        functools.partial(kernel, nc, nd),
        out_shape=(
            jax.ShapeDtypeStruct(queries.shape, BF16),
            jax.ShapeDtypeStruct(queries.shape, BF16),
            jax.ShapeDtypeStruct(keys.shape, BF16),
            jax.ShapeDtypeStruct(values.shape, BF16),
            jax.ShapeDtypeStruct((1, D), F32),
            jax.ShapeDtypeStruct((1, D), F32),
        ),
        in_specs=[pl.BlockSpec(memory_space=pl.ANY)] * 7,
        out_specs=(pl.BlockSpec(memory_space=pl.ANY),) * 6,
        scratch_shapes=[
            pltpu.VMEM((T, HEADS * D), BF16),
            pltpu.VMEM((T, KV * D), BF16),
            pltpu.VMEM((T, HEADS * D), BF16),
            pltpu.VMEM((1, D), F32),
            pltpu.VMEM((1, D), F32),
            pltpu.VMEM((1, T), jnp.int32),
            dma((2 * KV + 5,)),
            pltpu.VMEM((T, HEADS * D), BF16),
            pltpu.VMEM((T, HEADS * D), BF16),
            pltpu.VMEM((T, KV * D), BF16),
            pltpu.VMEM((T, KV * D), BF16),
            pltpu.VMEM((1, D), F32),
            pltpu.VMEM((1, D), F32),
            dma((4, KV)), dma((2,)),
            pltpu.VMEM((KV, (HALO + 1) * T, 2 * D), BF16),
            pltpu.VMEM((HALO + 1, 8, T), jnp.int32),
            pltpu.VMEM((KV, HALO * T, 2 * D), BF16),
            pltpu.VMEM((HALO, KV, T, 2 * D), BF16),
            pltpu.VMEM((KV, T, 2 * D), F32),
            pltpu.VMEM((2, D), F32),
            pltpu.VMEM((nc * nd - 1, 2, D), F32),
            dma((HALO, KV)), dma((HALO, KV)),
            dma((HALO,)), dma((HALO,)),
            dma((HALO, KV)), dma((HALO, KV)),
            dma, dma,
        ],
        compiler_params=pltpu.CompilerParams(
            collective_id=0, has_side_effects=True, vmem_limit_bytes=63 * 1024 * 1024,
        ),
    )(queries, keys, values, q_gain.reshape(1, D), key_norm_gain.reshape(1, D), segment_ids, output_gradient)
    attn_out, dq, dk, dv, gq, gk = deliver(*outs)
    return attn_out, dq, dk, dv, gq.reshape(D), gk.reshape(D)


def solution(mesh):
    tokens = P("dp", "ctx", None)
    return jax.shard_map(
        functools.partial(body, mesh.shape["ctx"], mesh.shape["dp"]),
        mesh=mesh,
        in_specs=(tokens, tokens, tokens, P(), P(), P("dp", "ctx"), tokens),
        out_specs=(tokens, tokens, tokens, tokens, P(), P()),
        check_vma=False,
    )
```

```python
import functools

import jax
import jax.numpy as jnp
from jax import lax
from jax.experimental import pallas as pl
from jax.experimental.pallas import tpu as pltpu
from jax.sharding import PartitionSpec as P

HEADS = 8
KV = 4
D = 256
WINDOW = 256
HALO = 2
EPS = 1e-06
SCALE = D ** (-0.5)
MESH = pl.DeviceIdType.MESH
F32 = jnp.float32
BF16 = jnp.bfloat16


def dot(a, b, contract):
    return lax.dot_general(a, b, ((contract[:1], contract[1:]), ((), ())), preferred_element_type=F32)


def hat(x):
    x = x.astype(F32)
    inv = lax.rsqrt(jnp.mean(x * x, -1, keepdims=True) + EPS)
    return x * inv, inv


def norm_backward(up, normed, inv, gain):
    g = up * gain
    return inv * (g - normed * jnp.mean(g * normed, -1, keepdims=True))


def kernel(
    nc, nd,
    q_hbm, k_hbm, v_hbm, qg_hbm, kg_hbm, seg_hbm, do_hbm,
    o_hbm, dq_hbm, dk_hbm, dv_hbm, gq_hbm, gk_hbm,
    q_ref, k_ref, do_ref, qg_ref, kg_ref, seg_ref, in_sem,
    o_ref, dq_ref, dk_ref, dv_ref, gq_ref, gk_ref, out_sem, gain_sem,
    kvbuf, segbuf, gbuf, grecv, own, far, part, stage,
    kv_send, kv_recv, seg_send, seg_recv, g_send, g_recv, r_send, r_recv,
):
    T = k_hbm.shape[1]
    me = lax.axis_index("ctx")
    dpi = lax.axis_index("dp")
    even = lax.rem(me, 2) == 0
    odd = lax.rem(me, 2) == 1
    middle = odd & (me > HALO)

    loads = {}

    def load(name, src, dst):
        loads[name] = pltpu.make_async_copy(src, dst, in_sem.at[len(loads)])
        loads[name].start()

    stores = []

    def store(src, dst, sem):
        stores.append(pltpu.make_async_copy(src, dst, sem))
        stores[-1].start()

    def arrive(name):
        loads[name].wait()

    load("kg", kg_hbm, kg_ref)
    for g in range(KV):
        col = pl.ds(g * D, D)
        load(f"k{g}", k_hbm.at[0, :, col], k_ref.at[:, col])
        load(f"v{g}", v_hbm.at[0, :, col], kvbuf.at[g, pl.ds(HALO * T, T), pl.ds(D, D)])
    load("seg", seg_hbm, seg_ref)
    load("qg", qg_hbm, qg_ref)
    load("q", q_hbm.at[0], q_ref)
    load("do", do_hbm.at[0], do_ref)

    barrier = pltpu.get_barrier_semaphore()

    rank = me * nd + dpi

    def peer_of(d):
        other = lax.rem(rank + d, nc * nd)
        return {"ctx": other // nd, "dp": lax.rem(other, nd)}

    @pl.loop(1, nc * nd)
    def _(d):
        pl.semaphore_signal(barrier, inc=1, device_id=peer_of(d), device_id_type=MESH)

    def remote(src, dst, send, recv, peer):
        return pltpu.make_async_remote_copy(
            src_ref=src, dst_ref=dst, send_sem=send, recv_sem=recv,
            device_id=peer, device_id_type=MESH,
        )

    def rows(block):
        return pl.ds(block * T, T)

    def kv_copy(g, off):
        return remote(
            kvbuf.at[g, rows(HALO)], kvbuf.at[g, rows(HALO - off)],
            kv_send.at[off - 1, g], kv_recv.at[off - 1, g], {"ctx": me + off},
        )

    def seg_copy(off):
        return remote(
            segbuf.at[HALO], segbuf.at[HALO - off],
            seg_send.at[off - 1], seg_recv.at[off - 1], {"ctx": me + off},
        )

    def sum_copy(d):
        return remote(part, stage.at[d - 1], r_send, r_recv, peer_of(d))

    def relay_copy(g):
        return remote(
            kvbuf.at[g, rows(0)], kvbuf.at[g, rows(1)], kv_send.at[0, g], kv_recv.at[0, g], {"ctx": me - 1},
        )

    def near_copy(g, to):
        return remote(
            gbuf.at[g, rows(1)], grecv.at[0, g], g_send.at[0, g], g_recv.at[0, g], {"ctx": me + to},
        )

    def far_copy(g):
        return remote(
            gbuf.at[g, rows(0)], grecv.at[1, g], g_send.at[1, g], g_recv.at[1, g], {"ctx": me - 2},
        )

    def pass_on(g):
        @pl.when(middle)
        def _():
            near_copy(g, 1).wait_recv()
            gbuf[g, rows(0)] = (far[g] + grecv[0, g].astype(F32)).astype(BF16)
            far_copy(g).start()

    arrive("kg")
    k_gain = kg_ref[...]
    for g in range(KV):
        col = pl.ds(g * D, D)
        arrive(f"k{g}")
        kvbuf[g, rows(HALO), 0:D] = (hat(k_ref[:, col])[0] * k_gain).astype(BF16)
        arrive(f"v{g}")
        if g == 0:
            arrive("seg")
            seg_row = seg_ref[...]
            segbuf[HALO] = jnp.broadcast_to(seg_row, (8, T))
            pl.semaphore_wait(barrier, nc * nd - 1)
            for off in range(1, HALO + 1):
                @pl.when(me + off < nc)
                def _(off=off):
                    seg_copy(off).start()

        @pl.when(me + 2 < nc)
        def _(g=g):
            kv_copy(g, 2).start()

        @pl.when(even)
        def _(g=g):
            kv_copy(g, 1).start()

    for off in range(1, HALO + 1):
        @pl.when(me < off)
        def _(off=off):
            for g in range(KV):
                kvbuf[g, rows(HALO - off)] = jnp.zeros((T, 2 * D), BF16)
            segbuf[HALO - off] = jnp.full((8, T), -1, jnp.int32)

    @pl.when(me + 2 >= nc)
    def _():
        for g in range(KV):
            grecv[1, g] = jnp.zeros((T, 2 * D), BF16)

    arrive("qg")
    q_gain = qg_ref[...]
    arrive("q")
    qs = []
    for h in range(HEADS):
        q_hat, _ = hat(q_ref[:, pl.ds(h * D, D)])
        qs.append((q_hat * q_gain).astype(BF16) * jnp.asarray(SCALE, BF16))

    seg_q = jnp.broadcast_to(seg_row, (T, T)).T
    for off in range(1, HALO + 1):
        @pl.when(me >= off)
        def _(off=off):
            seg_copy(off).wait_recv()
    qi = lax.broadcasted_iota(jnp.int32, (T, T), 0)
    ki = lax.broadcasted_iota(jnp.int32, (T, T), 1)
    masks = []
    for block in range(HALO + 1):
        dist = qi - ki + (HALO - block) * T
        same = seg_q == jnp.broadcast_to(segbuf[block, 0:1, :], (T, T))
        masks.append((dist >= 0) & (dist < WINDOW) & same)
    mask = jnp.concatenate(masks, 1)
    mask = jnp.concatenate([mask, mask], 0)

    arrive("do")
    gq = jnp.zeros((1, D), F32)
    gk = jnp.zeros((1, D), F32)
    for g in range(KV):
        @pl.when(me >= 2)
        def _(g=g):
            kv_copy(g, 2).wait_recv()

        @pl.when(middle)
        def _(g=g):
            relay_copy(g).start()

        @pl.when(me >= 1)
        def _(g=g):
            kv_copy(g, 1).wait_recv()
        K = kvbuf[g, :, 0:D]
        V = kvbuf[g, :, D:]
        Q = jnp.concatenate([qs[2 * g], qs[2 * g + 1]], 0)
        dO = jnp.concatenate(
            [do_ref[:, pl.ds(2 * g * D, D)], do_ref[:, pl.ds((2 * g + 1) * D, D)]], 0
        )
        E = jnp.where(mask, jnp.exp(dot(Q, K, (1, 1))), 0.0)
        prob = E * (1.0 / jnp.sum(E, -1, keepdims=True))
        prob_b = prob.astype(BF16)
        out = dot(prob_b, V, (1, 0)).astype(BF16)
        for i in range(2):
            o_ref[:, pl.ds((2 * g + i) * D, D)] = out[i * T:(i + 1) * T]
        delta = jnp.sum(dO.astype(F32) * out.astype(F32), -1, keepdims=True)
        ds = (prob * (dot(dO, V, (1, 1)) - delta)).astype(BF16)
        dK = dot(ds, Q, (0, 0))
        dV = dot(prob_b, dO, (0, 0))
        gbuf[g, rows(1), 0:D] = dK[T:2 * T].astype(BF16)
        gbuf[g, rows(1), D:] = dV[T:2 * T].astype(BF16)

        @pl.when(even & (me >= 2))
        def _(g=g, dK=dK, dV=dV):
            near_copy(g, 1).start()
            gbuf[g, rows(0), 0:D] = dK[:T].astype(BF16)
            gbuf[g, rows(0), D:] = dV[:T].astype(BF16)
            far_copy(g).start()

        @pl.when(odd)
        def _(g=g, dK=dK, dV=dV):
            near_copy(g, -1).start()
            far[g, :, 0:D] = dK[:T]
            far[g, :, D:] = dV[:T]

        own[g, :, 0:D] = dK[HALO * T:]
        own[g, :, D:] = dV[HALO * T:]
        gk += jnp.sum(dK * K.astype(F32), 0, keepdims=True)
        dQ = dot(ds, K, (1, 0)) * SCALE
        for i in range(2):
            col = pl.ds((2 * g + i) * D, D)
            q_hat, q_inv = hat(q_ref[:, col])
            up = dQ[i * T:(i + 1) * T]
            gq += jnp.sum(up * q_hat, 0, keepdims=True)
            dq_ref[:, col] = norm_backward(up, q_hat, q_inv, q_gain).astype(BF16)
        pair = pl.ds(2 * g * D, 2 * D)
        store(o_ref.at[:, pair], o_hbm.at[0, :, pair], out_sem.at[0, g])
        store(dq_ref.at[:, pair], dq_hbm.at[0, :, pair], out_sem.at[1, g])
        if g > 0:
            pass_on(g - 1)

    part[0:1, :] = gq
    part[1:2, :] = gk / k_gain

    @pl.loop(1, nc * nd)
    def _(d):
        sum_copy(d).start()

    pass_on(KV - 1)

    for g in range(KV):
        @pl.when(even)
        def _(g=g):
            near_copy(g, -1).wait_recv()

        @pl.when(me + 2 < nc)
        def _(g=g):
            far_copy(g).wait_recv()
        col = pl.ds(g * D, D)
        acc = own[g] + jnp.where(even, grecv[0, g].astype(F32), 0.0) + grecv[1, g].astype(F32)
        k_hat, k_inv = hat(k_ref[:, col])
        dk_ref[:, col] = norm_backward(acc[:, 0:D], k_hat, k_inv, k_gain).astype(BF16)
        dv_ref[:, col] = acc[:, D:].astype(BF16)
        store(dk_ref.at[:, col], dk_hbm.at[0, :, col], out_sem.at[2, g])
        store(dv_ref.at[:, col], dv_hbm.at[0, :, col], out_sem.at[3, g])

    for off in range(1, HALO + 1):
        @pl.when(me + off < nc)
        def _(off=off):
            seg_copy(off).wait_send()

    @pl.when(me + 2 < nc)
    def _():
        for g in range(KV):
            kv_copy(g, 2).wait_send()

    @pl.when(even | middle)
    def _():
        for g in range(KV):
            kv_copy(g, 1).wait_send()

    @pl.when(me >= 2)
    def _():
        for g in range(KV):
            far_copy(g).wait_send()

    @pl.when(me >= 1)
    def _():
        for g in range(KV):
            near_copy(g, 1).wait_send()

    pltpu.make_async_copy(stage, stage, r_send).wait()
    pltpu.make_async_copy(stage, stage, r_recv).wait()
    total = (part[...] + jnp.sum(stage[...], 0)) * float(nc * nd * T) ** (-0.5)
    gq_ref[...] = total[0:1]
    gk_ref[...] = total[1:2]
    store(gq_ref, gq_hbm, gain_sem.at[0])
    store(gk_ref, gk_hbm, gain_sem.at[1])
    for copy in stores:
        copy.wait()


def deliver_kernel(*refs):
    n = (len(refs) - 2) // 3
    ins, outs, held = refs[:n], refs[n:2 * n], refs[2 * n:3 * n]
    in_sem, out_sem = refs[-2:]
    loads = [pltpu.make_async_copy(ins[i], held[i], in_sem.at[i]) for i in range(n)]
    stores = [pltpu.make_async_copy(held[i], outs[i], out_sem.at[i]) for i in range(n)]
    for copy in loads:
        copy.start()
    for i in range(n):
        loads[i].wait()
        stores[i].start()
    for copy in stores:
        copy.wait()


def deliver(*arrays):
    n = len(arrays)
    anywhere = pl.BlockSpec(memory_space=pl.ANY)
    return pl.pallas_call(
        deliver_kernel,
        out_shape=tuple(jax.ShapeDtypeStruct(a.shape, a.dtype) for a in arrays),
        in_specs=[anywhere] * n,
        out_specs=(anywhere,) * n,
        scratch_shapes=[pltpu.VMEM(a.shape, a.dtype) for a in arrays]
        + [pltpu.SemaphoreType.DMA((n,))] * 2,
        compiler_params=pltpu.CompilerParams(vmem_limit_bytes=63 * 1024 * 1024),
    )(*arrays)


def body(nc, nd, queries, keys, values, q_gain, key_norm_gain, segment_ids, output_gradient):
    T = queries.shape[1]
    dma = pltpu.SemaphoreType.DMA
    outs = pl.pallas_call(
        functools.partial(kernel, nc, nd),
        out_shape=(
            jax.ShapeDtypeStruct(queries.shape, BF16),
            jax.ShapeDtypeStruct(queries.shape, BF16),
            jax.ShapeDtypeStruct(keys.shape, BF16),
            jax.ShapeDtypeStruct(values.shape, BF16),
            jax.ShapeDtypeStruct((1, D), F32),
            jax.ShapeDtypeStruct((1, D), F32),
        ),
        in_specs=[pl.BlockSpec(memory_space=pl.ANY)] * 7,
        out_specs=(pl.BlockSpec(memory_space=pl.ANY),) * 6,
        scratch_shapes=[
            pltpu.VMEM((T, HEADS * D), BF16),
            pltpu.VMEM((T, KV * D), BF16),
            pltpu.VMEM((T, HEADS * D), BF16),
            pltpu.VMEM((1, D), F32),
            pltpu.VMEM((1, D), F32),
            pltpu.VMEM((1, T), jnp.int32),
            dma((2 * KV + 5,)),
            pltpu.VMEM((T, HEADS * D), BF16),
            pltpu.VMEM((T, HEADS * D), BF16),
            pltpu.VMEM((T, KV * D), BF16),
            pltpu.VMEM((T, KV * D), BF16),
            pltpu.VMEM((1, D), F32),
            pltpu.VMEM((1, D), F32),
            dma((4, KV)), dma((2,)),
            pltpu.VMEM((KV, (HALO + 1) * T, 2 * D), BF16),
            pltpu.VMEM((HALO + 1, 8, T), jnp.int32),
            pltpu.VMEM((KV, HALO * T, 2 * D), BF16),
            pltpu.VMEM((HALO, KV, T, 2 * D), BF16),
            pltpu.VMEM((KV, T, 2 * D), F32),
            pltpu.VMEM((KV, T, 2 * D), F32),
            pltpu.VMEM((2, D), F32),
            pltpu.VMEM((nc * nd - 1, 2, D), F32),
            dma((HALO, KV)), dma((HALO, KV)),
            dma((HALO,)), dma((HALO,)),
            dma((HALO, KV)), dma((HALO, KV)),
            dma, dma,
        ],
        compiler_params=pltpu.CompilerParams(
            collective_id=0, has_side_effects=True, vmem_limit_bytes=63 * 1024 * 1024,
        ),
    )(queries, keys, values, q_gain.reshape(1, D), key_norm_gain.reshape(1, D), segment_ids, output_gradient)
    attn_out, dq, dk, dv, gq, gk = deliver(*outs)
    return attn_out, dq, dk, dv, gq.reshape(D), gk.reshape(D)


def solution(mesh):
    tokens = P("dp", "ctx", None)
    return jax.shard_map(
        functools.partial(body, mesh.shape["ctx"], mesh.shape["dp"]),
        mesh=mesh,
        in_specs=(tokens, tokens, tokens, P(), P(), P("dp", "ctx"), tokens),
        out_specs=(tokens, tokens, tokens, tokens, P(), P()),
        check_vma=False,
    )
```
